32 devices in a mesh: dom: 8 (over z, y), rep: 4 (over x, core).
Axes of the slice: x: 2, y: 2, z: 4, core: 2. Of those that a mesh axis runs over, the one named last changes fastest.
Arguments:
- profiles: bfloat16 [300, 8192], P(None, 'dom'), may hold values from -6 to 6
- pack_index: int32 [8, 4, 8, 16], P('dom', 'rep'), may hold values from 0 to 1023, as said below
- obs_slot: int32 [4, 16384], P(None, ('dom', 'rep')), may hold values from 0 to 127, as said below
- interp_weight: float32 [4, 16384], P(None, ('dom', 'rep')), may hold values from 0 to 1, as said below
- departures: float32 [100, 16384], P(None, ('dom', 'rep')), may hold values from -6 to 6
- w_in: bfloat16 [300, 512], replicated, may hold values from -0.375 to 0.375
- b_in: float32 [512], replicated, may hold values from -4 to 4
- w_mid: bfloat16 [512, 512], replicated, may hold values from -0.25 to 0.25
- b_mid: float32 [512], replicated, may hold values from -4 to 4
- w_out: bfloat16 [512, 100], replicated, may hold values from -0.25 to 0.25
Outputs:
- column_adjoint: float32 [300, 8192], P(None, ('dom', 'rep'))
The draws below stay inside these ranges and needn't reach their ends.
Inputs may be any that keep to these rules, and one draw needn't show every extreme that they name: Local column numbers within the partition that holds pack_index's first index; the 16 columns of pack_index[o, r, d, :] are distinct and lie in quarter d % 4 of the partition, that is from (d % 4) * 256 to one less than (d % 4 + 1) * 256. `obs_slot`: slot o * 16 + j names the j-th column that the observation's segment and replica index take from partition o; where o lies more than 2 partitions from the segment's own index, counted cyclically, j < 4. `interp_weight`: bilinear weights: the four of an observation sum to one.
All inputs are finite; a program needn't handle non-finite values.
Results may differ from the reference program's by a relative error of at most 0.0057.
Values may be sent and summed in bfloat16 or wider, within the bound.
A program may use at most 64 MiB of HBM per device.

```python
import jax
import jax.numpy as jnp
from jax import lax

F = 300
H = 512
C = 100
COL_DEV = 1024
OBS_DEV = 512
CAP = 16
NEAR = 2
FAR = 4
NCOL = 8192
NOBS = 16384
N_DOM = 8
N_REP = 4


def draw_pack_index(key, part):
    key_base = jax.random.fold_in(key, 11)
    key_order = jax.random.fold_in(key, 12)
    quarter = COL_DEV // N_REP
    base = jax.random.randint(key_base, (N_DOM, N_REP, N_DOM, 1), 0, quarter)
    scores = jax.random.randint(key_order, (N_DOM, N_REP, N_DOM, CAP), 0, 65536) * CAP + jnp.arange(CAP, dtype=jnp.int32)
    order = jnp.argsort(scores, axis=-1, stable=True).astype(jnp.int32)
    segment_quarter = (jnp.arange(N_DOM, dtype=jnp.int32) % N_REP).reshape(1, 1, N_DOM, 1)
    return ((base + order) % quarter + segment_quarter * quarter).astype(jnp.int32)


def draw_obs_slot(key, part):
    obs_index = jnp.arange(NOBS, dtype=jnp.int32)
    segment = obs_index // OBS_DEV // N_REP
    home_offset = jax.random.randint(jax.random.fold_in(key, 21), (NOBS,), -NEAR, NEAR + 1)
    choose = jax.random.randint(jax.random.fold_in(key, 22), (4, NOBS), 0, 2)
    far_owner = jax.random.randint(jax.random.fold_in(key, 23), (4, NOBS), 0, N_DOM)
    near_owner = (segment + home_offset) % N_DOM
    owner_index = jnp.where(choose == 0, near_owner[None, :], far_owner)
    apart = (owner_index - segment[None, :]) % N_DOM
    distance = jnp.minimum(apart, N_DOM - apart)
    limit = jnp.where(distance <= NEAR, CAP, FAR)
    within = jax.random.randint(jax.random.fold_in(key, 24), (4, NOBS), 0, 1048576) % limit
    return (owner_index * CAP + within).astype(jnp.int32)


def draw_interp_weight(key, part):
    key_east = jax.random.fold_in(key, 31)
    key_north = jax.random.fold_in(key, 32)
    east = jax.random.uniform(key_east, (NOBS,), jnp.float32, 0.05, 0.95)
    north = jax.random.uniform(key_north, (NOBS,), jnp.float32, 0.05, 0.95)
    stacked = jnp.stack([(1.0 - east) * (1.0 - north), east * (1.0 - north), (1.0 - east) * north, east * north])
    return stacked.astype(jnp.float32)


def shard_levels(rng, shape, shards, smallest, top_value):
    def one(position, blocks):
        draws = jax.random.uniform(jax.random.fold_in(jax.random.fold_in(rng, 6), position), (blocks,), jnp.float32, smallest / len(shards), top_value / len(shards))
        return jnp.repeat(jnp.exp(draws), shape[position] // blocks).reshape((-1,) + (1,) * (len(shape) - position - 1))

    gain = one(*shards[0])
    for cut in shards[1:]:
        gain = gain * one(*cut)
    return gain


def noise(own_key, extent, scale, bound, shards=(), kind=jnp.bfloat16):
    loudness = shard_levels(own_key, extent, shards, -0.22, 0.18) if shards else 1.0
    array = jax.random.normal(own_key, extent, jnp.float32) * scale * loudness
    return jnp.minimum(jnp.maximum(array, -bound), bound).astype(kind)


def setup_inputs(seed: int = 0) -> dict:
    key_list = jax.random.split(jax.random.key(seed), 11)
    profiles = noise(key_list[0], (F, NCOL), 1.0, 6.0, ((1, 8),))
    pack_index = draw_pack_index(jax.random.fold_in(key_list[10], 71), 0)
    obs_slot = draw_obs_slot(jax.random.fold_in(key_list[10], 71), 0)
    interp_weight = draw_interp_weight(jax.random.fold_in(key_list[10], 71), 0)
    departures = noise(key_list[4], (C, NOBS), 1.0, 6.0, ((1, 32),), jnp.float32)
    w_in = noise(key_list[5], (F, H), F ** -0.5, 0.375)
    b_in = noise(key_list[6], (H,), 1.0, 4.0, (), jnp.float32)
    w_mid = noise(key_list[7], (H, H), H ** -0.5, 0.25)
    b_mid = noise(key_list[8], (H,), 1.0, 4.0, (), jnp.float32)
    w_out = noise(key_list[9], (H, C), H ** -0.5, 0.25)
    return dict(profiles=profiles, pack_index=pack_index, obs_slot=obs_slot, interp_weight=interp_weight, departures=departures, w_in=w_in, b_in=b_in, w_mid=w_mid, b_mid=b_mid, w_out=w_out)


def stencil_columns(pack_index, obs_slot):
    obs_index = jnp.arange(NOBS, dtype=jnp.int32)
    device_index = obs_index // OBS_DEV
    segment = device_index // N_REP
    replica = device_index % N_REP
    owner_index = obs_slot // CAP
    within = obs_slot % CAP
    local_column = pack_index[owner_index, replica[None, :], segment[None, :], within]
    return (owner_index * COL_DEV + local_column).astype(jnp.int32)


def reference(profiles, pack_index, obs_slot, interp_weight, departures, w_in, b_in, w_mid, b_mid, w_out):
    column = stencil_columns(pack_index, obs_slot)
    block_count = NOBS // OBS_DEV
    column_blocks = column.reshape(4, block_count, OBS_DEV).transpose(1, 0, 2)
    weight_blocks = interp_weight.reshape(4, block_count, OBS_DEV).transpose(1, 0, 2)
    depart_blocks = departures.reshape(C, block_count, OBS_DEV).transpose(1, 0, 2)

    def advance(adjoint, block):
        columns_used, weights_used, depart_used = block
        summed = jnp.zeros((F, OBS_DEV), jnp.float32)
        for corner in range(4):
            summed = summed + weights_used[corner] * profiles[:, columns_used[corner]].astype(jnp.float32)
        inputs = summed.astype(jnp.bfloat16)
        z_one = jnp.dot(w_in.T, inputs, preferred_element_type=jnp.float32) + b_in[:, None]
        act_one = jnp.tanh(z_one).astype(jnp.bfloat16)
        z_two = jnp.dot(w_mid.T, act_one, preferred_element_type=jnp.float32) + b_mid[:, None]
        cot_out = depart_used.astype(jnp.bfloat16)
        g_two = (jnp.dot(w_out, cot_out, preferred_element_type=jnp.float32) * (1.0 - jnp.tanh(z_two) ** 2)).astype(jnp.bfloat16)
        g_one = (jnp.dot(w_mid, g_two, preferred_element_type=jnp.float32) * (1.0 - jnp.tanh(z_one) ** 2)).astype(jnp.bfloat16)
        g_inputs = jnp.dot(w_in, g_one, preferred_element_type=jnp.float32)
        for corner in range(4):
            adjoint = adjoint.at[:, columns_used[corner]].add(weights_used[corner] * g_inputs)
        return adjoint, None

    adjoint, _ = lax.scan(advance, jnp.zeros((F, NCOL), jnp.float32), (column_blocks, weight_blocks, depart_blocks))
    return adjoint
```

```python
import functools

import jax
import jax.numpy as jnp
from jax import lax
from jax.experimental import pallas as pl
from jax.experimental.pallas import tpu as pltpu
from jax.sharding import PartitionSpec as P

MESH = pl.DeviceIdType.MESH
F32 = jnp.float32
BF16 = jnp.bfloat16


def dot_nn(a, b):
    return lax.dot_general(a, b, (((1,), (0,)), ((), ())), preferred_element_type=F32)


def dot_nt(a, b):
    return lax.dot_general(a, b, (((1,), (1,)), ((), ())), preferred_element_type=F32)


def dot_tn(a, b):
    return lax.dot_general(a, b, (((0,), (0,)), ((), ())), preferred_element_type=F32)


def split_high_low(x):
    high = x.astype(BF16)
    return high, (x - high.astype(F32)).astype(BF16)


def pick_column(pick, table, cap):
    rows = pick.shape[0]
    spread = dot_nn(pick, table)
    lane = lax.broadcasted_iota(jnp.int32, (rows, cap), 1)
    row = lax.broadcasted_iota(jnp.int32, (rows, cap), 0)
    return jnp.sum(jnp.where(lane == row % cap, spread, 0.0), axis=1, keepdims=True)


def kernel(
    n_dom,
    n_rep,
    profiles_ref,
    pack_ref,
    slot_ref,
    weight_ref,
    departures_hbm,
    w_in_hbm,
    b_in_ref,
    w_mid_hbm,
    b_mid_ref,
    w_out_hbm,
    out_ref,
    departures_ref,
    w_in_ref,
    w_mid_ref,
    w_out_ref,
    send_fwd,
    fetched,
    index_all,
    spread_t,
    spread_s,
    g_out,
    send_bwd,
    returned,
    load_sem,
    idx_send,
    idx_recv,
    fwd_send,
    fwd_recv,
    bwd_send,
    bwd_recv,
):
    dom, rep = lax.axis_index("dom"), lax.axis_index("rep")
    cap = pack_ref.shape[1]
    per_rep = n_dom // n_rep
    slots = n_dom * cap
    feats = profiles_ref.shape[0]
    obs = slot_ref.shape[1]
    quarter = profiles_ref.shape[1] // n_rep
    my_part, my_group = dom % n_rep, dom // n_rep

    barrier = pltpu.get_barrier_semaphore()
    for step in range(1, n_rep):
        pl.semaphore_signal(
            barrier, inc=1, device_id=(dom, (rep + step) % n_rep), device_id_type=MESH
        )

    def greet(step, carry):
        pl.semaphore_signal(
            barrier, inc=1, device_id=((dom + step) % n_dom, rep), device_id_type=MESH
        )
        return carry

    lax.fori_loop(1, n_dom, greet, 0, unroll=n_dom <= 16)

    loads = [
        pltpu.make_async_copy(source, target, load_sem.at[k])
        for k, (source, target) in enumerate(
            (
                (departures_hbm, departures_ref),
                (w_out_hbm, w_out_ref),
                (w_in_hbm, w_in_ref),
                (w_mid_hbm, w_mid_ref),
            )
        )
    ]
    for load in loads:
        load.start()

    seg = lax.broadcasted_iota(jnp.int32, (n_dom, cap), 0)
    local = pack_ref[...] - (seg % n_rep) * quarter
    index_all[rep] = local
    row = lax.broadcasted_iota(jnp.int32, (slots, n_dom), 0) // cap
    col = lax.broadcasted_iota(jnp.int32, (slots, n_dom), 1)
    pick = (col == (row % per_rep) * n_rep + row // per_rep).astype(BF16)
    column = pick_column(pick, local.astype(BF16), cap).astype(jnp.int32)
    part_rows = per_rep * cap
    for part in range(n_rep):
        hot = (
            column[part * part_rows : (part + 1) * part_rows]
            == lax.broadcasted_iota(jnp.int32, (part_rows, quarter), 1)
        ).astype(BF16)
        packed = dot_nt(hot, profiles_ref[:, part * quarter : (part + 1) * quarter])
        send_fwd[part] = packed.astype(BF16).reshape(per_rep, cap, feats)

    pl.semaphore_wait(barrier, n_dom + n_rep - 2)

    def fwd_copy(step):
        peer = (dom + step) % n_dom
        return pltpu.make_async_remote_copy(
            src_ref=send_fwd.at[peer % n_rep, peer // n_rep],
            dst_ref=fetched.at[dom],
            send_sem=fwd_send.at[step],
            recv_sem=fwd_recv.at[step],
            device_id=(peer, rep),
            device_id_type=MESH,
        )

    def fwd_start(step, carry):
        fwd_copy(step).start()
        return carry

    lax.fori_loop(1, n_dom, fwd_start, 0, unroll=n_dom <= 16)

    idx_copies = [
        pltpu.make_async_remote_copy(
            src_ref=index_all.at[rep],
            dst_ref=index_all.at[rep],
            send_sem=idx_send.at[step],
            recv_sem=idx_recv.at[step],
            device_id=(dom, (rep + step) % n_rep),
            device_id_type=MESH,
        )
        for step in range(1, n_rep)
    ]
    for copy in idx_copies:
        copy.start()

    fetched[dom] = send_fwd[my_part, my_group]

    chunk = 128 if slots % 128 == 0 else slots

    def build(c, carry):
        first = pl.multiple_of(c * chunk, chunk)
        ids = lax.broadcasted_iota(jnp.int32, (chunk, obs), 0) + first
        total = jnp.zeros((chunk, obs), F32)
        for k in range(4):
            total = total + jnp.where(ids == slot_ref[k : k + 1, :], weight_ref[k : k + 1, :], 0.0)
        high, low = split_high_low(total)
        spread_s[0, pl.ds(first, chunk), :] = high
        spread_s[1, pl.ds(first, chunk), :] = low
        high_t, low_t = split_high_low(total.T)
        spread_t[:, pl.ds(first, chunk)] = high_t
        spread_t[:, pl.ds(pl.multiple_of(slots + first, chunk), chunk)] = low_t
        return carry

    lax.fori_loop(0, slots // chunk, build, 0, unroll=slots == chunk)

    loads[0].wait()
    loads[1].wait()
    g_out[...] = dot_nt(departures_ref[...].T.astype(BF16), w_out_ref[...])
    loads[2].wait()
    loads[3].wait()

    def fwd_wait(step, carry):
        fwd_copy(step).wait()
        return carry

    lax.fori_loop(1, n_dom, fwd_wait, 0, unroll=n_dom <= 16)

    columns = fetched[...].reshape(slots, feats)
    inputs = dot_nn(spread_t[...], jnp.concatenate([columns, columns], axis=0)).astype(BF16)
    act_one = jnp.tanh(dot_nn(inputs, w_in_ref[...]) + b_in_ref[...])
    act_two = jnp.tanh(dot_nn(act_one.astype(BF16), w_mid_ref[...]) + b_mid_ref[...])
    g_two = (g_out[...] * (1.0 - act_two * act_two)).astype(BF16)
    g_one = (dot_nt(g_two, w_mid_ref[...]) * (1.0 - act_one * act_one)).astype(BF16)
    hidden = dot_nn(spread_s[0], g_one) + dot_nn(spread_s[1], g_one)
    slot_adjoint = dot_nt(hidden.astype(BF16), w_in_ref[...])
    send_bwd[...] = slot_adjoint.astype(BF16).reshape(n_dom, cap, feats)

    def bwd_copy(step):
        owner = (dom + step) % n_dom
        return pltpu.make_async_remote_copy(
            src_ref=send_bwd.at[owner],
            dst_ref=returned.at[my_group * n_rep + rep],
            send_sem=bwd_send.at[step],
            recv_sem=bwd_recv.at[my_group * n_rep + rep],
            device_id=(owner, my_part),
            device_id_type=MESH,
        )

    def bwd_start(step, carry):
        bwd_copy(step).start()
        return carry

    lax.fori_loop(1, n_dom, bwd_start, 0, unroll=n_dom <= 16)

    @pl.when(my_part != rep)
    def _():
        bwd_copy(0).start()

    @pl.when(my_part == rep)
    def _():
        returned[my_group * n_rep + rep] = send_bwd[dom]

    for copy in idx_copies:
        copy.wait()
    table = index_all[...].astype(BF16).reshape(n_rep * n_dom, cap)
    row = lax.broadcasted_iota(jnp.int32, (slots, n_rep * n_dom), 0) // cap
    col = lax.broadcasted_iota(jnp.int32, (slots, n_rep * n_dom), 1)
    pick = (col == (row % n_rep) * n_dom + (row // n_rep) * n_rep + rep).astype(BF16)
    target = pick_column(pick, table, cap).astype(jnp.int32)
    hot = (target == lax.broadcasted_iota(jnp.int32, (slots, quarter), 1)).astype(BF16)

    def bwd_wait(sender, carry):
        from_dom = (sender // n_rep) * n_rep + rep
        from_rep = sender % n_rep

        @pl.when(jnp.logical_or(from_dom != dom, from_rep != rep))
        def _():
            pltpu.make_async_remote_copy(
                src_ref=send_bwd.at[0],
                dst_ref=returned.at[sender],
                send_sem=bwd_send.at[0],
                recv_sem=bwd_recv.at[sender],
                device_id=(from_dom, from_rep),
                device_id_type=MESH,
            ).wait_recv()

        return carry

    lax.fori_loop(0, n_dom, bwd_wait, 0, unroll=n_dom <= 16)

    out_ref[...] = dot_tn(returned[...].reshape(slots, feats), hot)

    def bwd_sent(step, carry):
        bwd_copy(step).wait_send()
        return carry

    lax.fori_loop(1, n_dom, bwd_sent, 0, unroll=n_dom <= 16)

    @pl.when(my_part != rep)
    def _():
        bwd_copy(0).wait_send()


def body(
    n_dom,
    n_rep,
    profiles,
    pack_index,
    obs_slot,
    interp_weight,
    departures,
    w_in,
    b_in,
    w_mid,
    b_mid,
    w_out,
):
    feats, width = profiles.shape
    cap = pack_index.shape[3]
    slots = n_dom * cap
    obs = obs_slot.shape[1]
    hidden = w_in.shape[1]
    vmem = pl.BlockSpec(memory_space=pltpu.VMEM)
    hbm = pl.BlockSpec(memory_space=pl.ANY)
    return pl.pallas_call(
        functools.partial(kernel, n_dom, n_rep),
        out_shape=jax.ShapeDtypeStruct((feats, width // n_rep), F32),
        in_specs=[vmem, vmem, vmem, vmem, hbm, hbm, vmem, hbm, vmem, hbm],
        out_specs=vmem,
        scratch_shapes=[
            pltpu.VMEM(departures.shape, F32),
            pltpu.VMEM(w_in.shape, BF16),
            pltpu.VMEM(w_mid.shape, BF16),
            pltpu.VMEM(w_out.shape, BF16),
            pltpu.VMEM((n_rep, n_dom // n_rep, cap, feats), BF16),
            pltpu.VMEM((n_dom, cap, feats), BF16),
            pltpu.VMEM((n_rep, n_dom, cap), jnp.int32),
            pltpu.VMEM((obs, 2 * slots), BF16),
            pltpu.VMEM((2, slots, obs), BF16),
            pltpu.VMEM((obs, hidden), F32),
            pltpu.VMEM((n_dom, cap, feats), BF16),
            pltpu.VMEM((n_dom, cap, feats), BF16),
            pltpu.SemaphoreType.DMA((4,)),
            pltpu.SemaphoreType.DMA((n_rep,)),
            pltpu.SemaphoreType.DMA((n_rep,)),
            pltpu.SemaphoreType.DMA((n_dom,)),
            pltpu.SemaphoreType.DMA((n_dom,)),
            pltpu.SemaphoreType.DMA((n_dom,)),
            pltpu.SemaphoreType.DMA((n_dom,)),
        ],
        compiler_params=pltpu.CompilerParams(
            collective_id=0, has_side_effects=True, vmem_limit_bytes=48 * 1024 * 1024
        ),
    )(
        profiles,
        pack_index.reshape(n_dom, cap),
        obs_slot,
        interp_weight,
        departures,
        w_in,
        b_in.reshape(1, hidden),
        w_mid,
        b_mid.reshape(1, hidden),
        w_out,
    )


def solution(mesh):
    placed = (
        P(None, "dom"),
        P("dom", "rep", None, None),
        P(None, ("dom", "rep")),
        P(None, ("dom", "rep")),
        P(None, ("dom", "rep")),
        P(),
        P(),
        P(),
        P(),
        P(),
    )
    return jax.shard_map(
        functools.partial(body, mesh.shape["dom"], mesh.shape["rep"]),
        mesh=mesh,
        in_specs=placed,
        out_specs=P(None, ("dom", "rep")),
        check_vma=False,
    )
```

```python
import functools

import jax
import jax.numpy as jnp
from jax import lax
from jax.experimental import pallas as pl
from jax.experimental.pallas import tpu as pltpu
from jax.sharding import PartitionSpec as P

MESH = pl.DeviceIdType.MESH
F32 = jnp.float32
BF16 = jnp.bfloat16


def dot_nn(a, b):
    return lax.dot_general(a, b, (((1,), (0,)), ((), ())), preferred_element_type=F32)


def dot_nt(a, b):
    return lax.dot_general(a, b, (((1,), (1,)), ((), ())), preferred_element_type=F32)


def dot_tn(a, b):
    return lax.dot_general(a, b, (((0,), (0,)), ((), ())), preferred_element_type=F32)


def split_high_low(x):
    high = x.astype(BF16)
    return high, (x - high.astype(F32)).astype(BF16)


def pick_column(pick, table, cap):
    rows = pick.shape[0]
    spread = dot_nn(pick, table)
    lane = lax.broadcasted_iota(jnp.int32, (rows, cap), 1)
    row = lax.broadcasted_iota(jnp.int32, (rows, cap), 0)
    return jnp.sum(jnp.where(lane == row % cap, spread, 0.0), axis=1, keepdims=True)


def kernel(
    n_dom,
    n_rep,
    profiles_hbm,
    pack_hbm,
    slot_hbm,
    weight_hbm,
    departures_hbm,
    w_in_hbm,
    b_in_hbm,
    w_mid_hbm,
    b_mid_hbm,
    w_out_t_hbm,
    out_ref,
    profiles_ref,
    pack_ref,
    slot_ref,
    weight_ref,
    departures_ref,
    w_in_ref,
    b_in_ref,
    w_mid_ref,
    b_mid_ref,
    w_out_t_ref,
    send_fwd,
    fetched,
    index_all,
    spread_t,
    spread_s,
    g_out,
    send_bwd,
    returned,
    load_sem,
    idx_send,
    idx_recv,
    fwd_send,
    fwd_recv,
    bwd_send,
    bwd_recv,
):
    dom, rep = lax.axis_index("dom"), lax.axis_index("rep")
    cap = pack_ref.shape[1]
    per_rep = n_dom // n_rep
    slots = n_dom * cap
    feats = profiles_ref.shape[0]
    obs = slot_ref.shape[1]
    quarter = profiles_ref.shape[1] // n_rep
    my_part, my_group = dom % n_rep, dom // n_rep

    loads = [
        pltpu.make_async_copy(source, target, load_sem.at[k])
        for k, (source, target) in enumerate(
            (
                (pack_hbm, pack_ref),
                (profiles_hbm, profiles_ref),
                (slot_hbm, slot_ref),
                (weight_hbm, weight_ref),
                (departures_hbm, departures_ref),
                (w_out_t_hbm, w_out_t_ref),
                (w_in_hbm, w_in_ref),
                (b_in_hbm, b_in_ref),
                (w_mid_hbm, w_mid_ref),
                (b_mid_hbm, b_mid_ref),
            )
        )
    ]
    for load in loads:
        load.start()

    barrier = pltpu.get_barrier_semaphore()
    for step in range(1, n_rep):
        pl.semaphore_signal(
            barrier, inc=1, device_id=(dom, (rep + step) % n_rep), device_id_type=MESH
        )

    def greet(step, carry):
        pl.semaphore_signal(
            barrier, inc=1, device_id=((dom + step) % n_dom, rep), device_id_type=MESH
        )
        return carry

    lax.fori_loop(1, n_dom, greet, 0, unroll=n_dom <= 16)

    loads[0].wait()
    seg = lax.broadcasted_iota(jnp.int32, (n_dom, cap), 0)
    local = pack_ref[...] - (seg % n_rep) * quarter
    index_all[rep] = local
    row = lax.broadcasted_iota(jnp.int32, (slots, n_dom), 0) // cap
    col = lax.broadcasted_iota(jnp.int32, (slots, n_dom), 1)
    pick = (col == (row % per_rep) * n_rep + row // per_rep).astype(BF16)
    column = pick_column(pick, local.astype(BF16), cap).astype(jnp.int32)
    part_rows = per_rep * cap
    loads[1].wait()
    for part in range(n_rep):
        hot = (
            column[part * part_rows : (part + 1) * part_rows]
            == lax.broadcasted_iota(jnp.int32, (part_rows, quarter), 1)
        ).astype(BF16)
        packed = dot_nt(hot, profiles_ref[:, part * quarter : (part + 1) * quarter])
        send_fwd[part] = packed.astype(BF16).reshape(per_rep, cap, feats)

    pl.semaphore_wait(barrier, n_dom + n_rep - 2)

    def fwd_copy(step):
        peer = (dom + step) % n_dom
        return pltpu.make_async_remote_copy(
            src_ref=send_fwd.at[peer % n_rep, peer // n_rep],
            dst_ref=fetched.at[dom],
            send_sem=fwd_send.at[step],
            recv_sem=fwd_recv.at[step],
            device_id=(peer, rep),
            device_id_type=MESH,
        )

    def fwd_start(step, carry):
        fwd_copy(step).start()
        return carry

    lax.fori_loop(1, n_dom, fwd_start, 0, unroll=n_dom <= 16)

    idx_copies = [
        pltpu.make_async_remote_copy(
            src_ref=index_all.at[rep],
            dst_ref=index_all.at[rep],
            send_sem=idx_send.at[step],
            recv_sem=idx_recv.at[step],
            device_id=(dom, (rep + step) % n_rep),
            device_id_type=MESH,
        )
        for step in range(1, n_rep)
    ]
    for copy in idx_copies:
        copy.start()

    fetched[dom] = send_fwd[my_part, my_group]

    loads[2].wait()
    loads[3].wait()
    chunk = 128 if slots % 128 == 0 else slots

    def build(c, carry):
        first = pl.multiple_of(c * chunk, chunk)
        ids = lax.broadcasted_iota(jnp.int32, (chunk, obs), 0) + first
        total = jnp.zeros((chunk, obs), F32)
        for k in range(4):
            total = total + jnp.where(ids == slot_ref[k : k + 1, :], weight_ref[k : k + 1, :], 0.0)
        high, low = split_high_low(total)
        spread_s[0, pl.ds(first, chunk), :] = high
        spread_s[1, pl.ds(first, chunk), :] = low
        high_t, low_t = split_high_low(total.T)
        spread_t[:, pl.ds(first, chunk)] = high_t
        spread_t[:, pl.ds(pl.multiple_of(slots + first, chunk), chunk)] = low_t
        return carry

    lax.fori_loop(0, slots // chunk, build, 0, unroll=slots == chunk)

    loads[4].wait()
    loads[5].wait()
    g_out[...] = dot_nn(departures_ref[...].T.astype(BF16), w_out_t_ref[...])
    for load in loads[6:]:
        load.wait()

    def fwd_wait(step, carry):
        fwd_copy(step).wait()
        return carry

    lax.fori_loop(1, n_dom, fwd_wait, 0, unroll=n_dom <= 16)

    columns = fetched[...].reshape(slots, feats)
    inputs = dot_nn(spread_t[...], jnp.concatenate([columns, columns], axis=0)).astype(BF16)
    act_one = jnp.tanh(dot_nn(inputs, w_in_ref[...]) + b_in_ref[...])
    act_two = jnp.tanh(dot_nn(act_one.astype(BF16), w_mid_ref[...]) + b_mid_ref[...])
    g_two = (g_out[...] * (1.0 - act_two * act_two)).astype(BF16)
    g_one = (dot_nt(g_two, w_mid_ref[...]) * (1.0 - act_one * act_one)).astype(BF16)
    hidden = dot_nn(spread_s[0], g_one) + dot_nn(spread_s[1], g_one)
    slot_adjoint = dot_nt(hidden.astype(BF16), w_in_ref[...])
    send_bwd[...] = slot_adjoint.astype(BF16).reshape(n_dom, cap, feats)

    def bwd_copy(step):
        owner = (dom + step) % n_dom
        return pltpu.make_async_remote_copy(
            src_ref=send_bwd.at[owner],
            dst_ref=returned.at[my_group * n_rep + rep],
            send_sem=bwd_send.at[step],
            recv_sem=bwd_recv.at[my_group * n_rep + rep],
            device_id=(owner, my_part),
            device_id_type=MESH,
        )

    def bwd_start(step, carry):
        bwd_copy(step).start()
        return carry

    lax.fori_loop(1, n_dom, bwd_start, 0, unroll=n_dom <= 16)

    @pl.when(my_part != rep)
    def _():
        bwd_copy(0).start()

    @pl.when(my_part == rep)
    def _():
        returned[my_group * n_rep + rep] = send_bwd[dom]

    for copy in idx_copies:
        copy.wait()
    table = index_all[...].astype(BF16).reshape(n_rep * n_dom, cap)
    row = lax.broadcasted_iota(jnp.int32, (slots, n_rep * n_dom), 0) // cap
    col = lax.broadcasted_iota(jnp.int32, (slots, n_rep * n_dom), 1)
    pick = (col == (row % n_rep) * n_dom + (row // n_rep) * n_rep + rep).astype(BF16)
    target = pick_column(pick, table, cap).astype(jnp.int32)
    hot = (target == lax.broadcasted_iota(jnp.int32, (slots, quarter), 1)).astype(BF16)

    def bwd_wait(sender, carry):
        from_dom = (sender // n_rep) * n_rep + rep
        from_rep = sender % n_rep

        @pl.when(jnp.logical_or(from_dom != dom, from_rep != rep))
        def _():
            pltpu.make_async_remote_copy(
                src_ref=send_bwd.at[0],
                dst_ref=returned.at[sender],
                send_sem=bwd_send.at[0],
                recv_sem=bwd_recv.at[sender],
                device_id=(from_dom, from_rep),
                device_id_type=MESH,
            ).wait_recv()

        return carry

    lax.fori_loop(0, n_dom, bwd_wait, 0, unroll=n_dom <= 16)

    out_ref[...] = dot_tn(returned[...].reshape(slots, feats), hot)

    def bwd_sent(step, carry):
        bwd_copy(step).wait_send()
        return carry

    lax.fori_loop(1, n_dom, bwd_sent, 0, unroll=n_dom <= 16)

    @pl.when(my_part != rep)
    def _():
        bwd_copy(0).wait_send()


def body(
    n_dom,
    n_rep,
    profiles,
    pack_index,
    obs_slot,
    interp_weight,
    departures,
    w_in,
    b_in,
    w_mid,
    b_mid,
    w_out,
):
    feats, width = profiles.shape
    cap = pack_index.shape[3]
    slots = n_dom * cap
    obs = obs_slot.shape[1]
    hidden = w_in.shape[1]
    vmem = pl.BlockSpec(memory_space=pltpu.VMEM)
    operands = (
        profiles,
        pack_index.reshape(n_dom, cap),
        obs_slot,
        interp_weight,
        departures,
        w_in,
        b_in.reshape(1, hidden),
        w_mid,
        b_mid.reshape(1, hidden),
        w_out.T,
    )
    return pl.pallas_call(
        functools.partial(kernel, n_dom, n_rep),
        out_shape=jax.ShapeDtypeStruct((feats, width // n_rep), F32),
        in_specs=[pl.BlockSpec(memory_space=pltpu.HBM)] * len(operands),
        out_specs=vmem,
        scratch_shapes=[
            *(pltpu.VMEM(operand.shape, operand.dtype) for operand in operands),
            pltpu.VMEM((n_rep, n_dom // n_rep, cap, feats), BF16),
            pltpu.VMEM((n_dom, cap, feats), BF16),
            pltpu.VMEM((n_rep, n_dom, cap), jnp.int32),
            pltpu.VMEM((obs, 2 * slots), BF16),
            pltpu.VMEM((2, slots, obs), BF16),
            pltpu.VMEM((obs, hidden), F32),
            pltpu.VMEM((n_dom, cap, feats), BF16),
            pltpu.VMEM((n_dom, cap, feats), BF16),
            pltpu.SemaphoreType.DMA((len(operands),)),
            pltpu.SemaphoreType.DMA((n_rep,)),
            pltpu.SemaphoreType.DMA((n_rep,)),
            pltpu.SemaphoreType.DMA((n_dom,)),
            pltpu.SemaphoreType.DMA((n_dom,)),
            pltpu.SemaphoreType.DMA((n_dom,)),
            pltpu.SemaphoreType.DMA((n_dom,)),
        ],
        compiler_params=pltpu.CompilerParams(
            collective_id=0, has_side_effects=True, vmem_limit_bytes=64 * 1024 * 1024
        ),
    )(*operands)


def solution(mesh):
    placed = (
        P(None, "dom"),
        P("dom", "rep", None, None),
        P(None, ("dom", "rep")),
        P(None, ("dom", "rep")),
        P(None, ("dom", "rep")),
        P(),
        P(),
        P(),
        P(),
        P(),
    )
    return jax.shard_map(
        functools.partial(body, mesh.shape["dom"], mesh.shape["rep"]),
        mesh=mesh,
        in_specs=placed,
        out_specs=P(None, ("dom", "rep")),
        check_vma=False,
    )
```

```python
import functools

import jax
import jax.numpy as jnp
from jax import lax
from jax.experimental import pallas as pl
from jax.experimental.pallas import tpu as pltpu
from jax.sharding import PartitionSpec as P

MESH = pl.DeviceIdType.MESH
F32 = jnp.float32
BF16 = jnp.bfloat16


def dot_nn(a, b):
    return lax.dot_general(a, b, (((1,), (0,)), ((), ())), preferred_element_type=F32)


def dot_nt(a, b):
    return lax.dot_general(a, b, (((1,), (1,)), ((), ())), preferred_element_type=F32)


def dot_tn(a, b):
    return lax.dot_general(a, b, (((0,), (0,)), ((), ())), preferred_element_type=F32)


def split_high_low(x):
    high = x.astype(BF16)
    return high, (x - high.astype(F32)).astype(BF16)


def pick_column(pick, table, cap):
    rows = pick.shape[0]
    spread = dot_nn(pick, table)
    lane = lax.broadcasted_iota(jnp.int32, (rows, cap), 1)
    row = lax.broadcasted_iota(jnp.int32, (rows, cap), 0)
    return jnp.sum(jnp.where(lane == row % cap, spread, 0.0), axis=1, keepdims=True)


def each(low, high, act):
    if high - low <= 16:
        for step in range(low, high):
            act(step)
    else:
        lax.fori_loop(low, high, lambda step, carry: (act(step), carry)[1], 0)


def partner(index, step, count):
    if count > 16 or count & (count - 1):
        return (index + step) % count
    bits, result = (count - step) % count, index
    for k in range(count.bit_length() - 1):
        if (bits >> k) & 1:
            result = result + (1 << k) * (1 - 2 * ((index // (1 << k)) % 2))
    return result


def kernel(
    n_dom,
    n_rep,
    profiles_hbm,
    pack_hbm,
    slot_hbm,
    weight_hbm,
    departures_hbm,
    w_in_hbm,
    b_in_hbm,
    w_mid_hbm,
    b_mid_hbm,
    w_out_t_hbm,
    out_ref,
    profiles_ref,
    pack_ref,
    slot_ref,
    weight_ref,
    departures_ref,
    w_in_ref,
    b_in_ref,
    w_mid_ref,
    b_mid_ref,
    w_out_t_ref,
    send_fwd,
    fetched,
    index_all,
    spread_t,
    spread_s,
    g_out,
    send_bwd,
    returned,
    load_sem,
    first_sem,
    idx_send,
    idx_recv,
    fwd_send,
    fwd_recv,
    bwd_send,
    bwd_recv,
):
    dom, rep = lax.axis_index("dom"), lax.axis_index("rep")
    cap = pack_ref.shape[1]
    per_rep = n_dom // n_rep
    slots = n_dom * cap
    feats = profiles_ref.shape[0]
    obs = slot_ref.shape[1]
    quarter = profiles_ref.shape[1] // n_rep
    my_part, my_group = dom % n_rep, dom // n_rep

    first_loads = [pltpu.make_async_copy(pack_hbm, pack_ref, load_sem.at[0])] + [
        pltpu.make_async_copy(
            profiles_hbm.at[:, pl.ds(part * quarter, quarter)],
            profiles_ref.at[:, pl.ds(part * quarter, quarter)],
            first_sem.at[part],
        )
        for part in range(n_rep)
    ]
    loads = [
        pltpu.make_async_copy(source, target, load_sem.at[k + 1])
        for k, (source, target) in enumerate(
            (
                (slot_hbm, slot_ref),
                (weight_hbm, weight_ref),
                (departures_hbm, departures_ref),
                (w_out_t_hbm, w_out_t_ref),
                (w_in_hbm, w_in_ref),
                (b_in_hbm, b_in_ref),
                (w_mid_hbm, w_mid_ref),
                (b_mid_hbm, b_mid_ref),
            )
        )
    ]
    for load in first_loads:
        load.start()

    barrier = pltpu.get_barrier_semaphore()
    for step in range(1, n_rep):
        pl.semaphore_signal(
            barrier, inc=1, device_id=(dom, (rep + step) % n_rep), device_id_type=MESH
        )

    def greet(step):
        pl.semaphore_signal(
            barrier, inc=1, device_id=(partner(dom, step, n_dom), rep), device_id_type=MESH
        )

    each(1, n_dom, greet)

    for load in loads:
        load.start()

    first_loads[0].wait()
    seg = lax.broadcasted_iota(jnp.int32, (n_dom, cap), 0)
    local = pack_ref[...] - (seg % n_rep) * quarter
    index_all[rep] = local
    row = lax.broadcasted_iota(jnp.int32, (slots, n_dom), 0) // cap
    col = lax.broadcasted_iota(jnp.int32, (slots, n_dom), 1)
    pick = (col == (row % per_rep) * n_rep + row // per_rep).astype(BF16)
    column = pick_column(pick, local.astype(BF16), cap).astype(jnp.int32)
    part_rows = per_rep * cap
    for part in range(n_rep):
        hot = (
            column[part * part_rows : (part + 1) * part_rows]
            == lax.broadcasted_iota(jnp.int32, (part_rows, quarter), 1)
        ).astype(BF16)
        first_loads[1 + part].wait()
        packed = dot_nt(hot, profiles_ref[:, part * quarter : (part + 1) * quarter])
        send_fwd[part] = packed.astype(BF16).reshape(per_rep, cap, feats)

    pl.semaphore_wait(barrier, n_dom + n_rep - 2)

    def fwd_copy(step):
        peer = partner(dom, step, n_dom)
        return pltpu.make_async_remote_copy(
            src_ref=send_fwd.at[peer % n_rep, peer // n_rep],
            dst_ref=fetched.at[dom],
            send_sem=fwd_send.at[step],
            recv_sem=fwd_recv.at[step],
            device_id=(peer, rep),
            device_id_type=MESH,
        )

    def fwd_start(step):
        fwd_copy(step).start()

    each(1, n_dom, fwd_start)

    idx_copies = [
        pltpu.make_async_remote_copy(
            src_ref=index_all.at[rep],
            dst_ref=index_all.at[rep],
            send_sem=idx_send.at[step],
            recv_sem=idx_recv.at[step],
            device_id=(dom, (rep + step) % n_rep),
            device_id_type=MESH,
        )
        for step in range(1, n_rep)
    ]
    for copy in idx_copies:
        copy.start()

    fetched[dom] = send_fwd[my_part, my_group]

    loads[0].wait()
    loads[1].wait()
    chunk = 128 if slots % 128 == 0 else slots

    def build(c, carry):
        first = pl.multiple_of(c * chunk, chunk)
        ids = lax.broadcasted_iota(jnp.int32, (chunk, obs), 0) + first
        total = jnp.zeros((chunk, obs), F32)
        for k in range(4):
            total = total + jnp.where(ids == slot_ref[k : k + 1, :], weight_ref[k : k + 1, :], 0.0)
        high, low = split_high_low(total)
        spread_s[pl.ds(first, chunk), :] = high
        spread_s[pl.ds(pl.multiple_of(slots + first, chunk), chunk), :] = low
        high_t, low_t = split_high_low(total.T)
        spread_t[:, pl.ds(first, chunk)] = high_t
        spread_t[:, pl.ds(pl.multiple_of(slots + first, chunk), chunk)] = low_t
        return carry

    lax.fori_loop(0, slots // chunk, build, 0, unroll=slots == chunk)

    loads[2].wait()
    loads[3].wait()
    g_out[...] = dot_nn(departures_ref[...].T.astype(BF16), w_out_t_ref[...])
    for load in loads[4:]:
        load.wait()

    def fwd_wait(step):
        fwd_copy(step).wait_recv()

    each(1, n_dom, fwd_wait)

    columns = fetched[...].reshape(slots, feats)
    inputs = dot_nn(spread_t[...], jnp.concatenate([columns, columns], axis=0)).astype(BF16)
    act_one = jnp.tanh(dot_nn(inputs, w_in_ref[...]) + b_in_ref[...])
    act_two = jnp.tanh(dot_nn(act_one.astype(BF16), w_mid_ref[...]) + b_mid_ref[...])
    g_two = (g_out[...] * (1.0 - act_two * act_two)).astype(BF16)
    g_one = (dot_nt(g_two, w_mid_ref[...]) * (1.0 - act_one * act_one)).astype(BF16)
    both = dot_nn(spread_s[...], g_one)
    hidden = both[:slots] + both[slots:]
    slot_adjoint = dot_nt(hidden.astype(BF16), w_in_ref[...])
    send_bwd[...] = slot_adjoint.astype(BF16).reshape(n_dom, cap, feats)

    def bwd_copy(step):
        owner = partner(dom, step, n_dom)
        return pltpu.make_async_remote_copy(
            src_ref=send_bwd.at[owner],
            dst_ref=returned.at[my_group * n_rep + rep],
            send_sem=bwd_send.at[step],
            recv_sem=bwd_recv.at[my_group * n_rep + rep],
            device_id=(owner, my_part),
            device_id_type=MESH,
        )

    def bwd_start(step):
        bwd_copy(step).start()

    each(1, n_dom, bwd_start)

    @pl.when(my_part != rep)
    def _():
        bwd_copy(0).start()

    @pl.when(my_part == rep)
    def _():
        returned[my_group * n_rep + rep] = send_bwd[dom]

    for copy in idx_copies:
        copy.wait()
    table = index_all[...].astype(BF16).reshape(n_rep * n_dom, cap)
    row = lax.broadcasted_iota(jnp.int32, (slots, n_rep * n_dom), 0) // cap
    col = lax.broadcasted_iota(jnp.int32, (slots, n_rep * n_dom), 1)
    pick = (col == (row % n_rep) * n_dom + (row // n_rep) * n_rep + rep).astype(BF16)
    target = pick_column(pick, table, cap).astype(jnp.int32)
    hot = (target == lax.broadcasted_iota(jnp.int32, (slots, quarter), 1)).astype(BF16)

    def bwd_wait(sender):
        from_dom = (sender // n_rep) * n_rep + rep
        from_rep = sender % n_rep

        @pl.when(jnp.logical_or(from_dom != dom, from_rep != rep))
        def _():
            pltpu.make_async_remote_copy(
                src_ref=send_bwd.at[0],
                dst_ref=returned.at[sender],
                send_sem=bwd_send.at[0],
                recv_sem=bwd_recv.at[sender],
                device_id=(from_dom, from_rep),
                device_id_type=MESH,
            ).wait_recv()


    each(0, n_dom, bwd_wait)

    out_ref[...] = dot_tn(returned[...].reshape(slots, feats), hot)

    def bwd_sent(step):
        bwd_copy(step).wait_send()

    each(1, n_dom, bwd_sent)
    each(1, n_dom, lambda step: fwd_copy(step).wait_send())

    @pl.when(my_part != rep)
    def _():
        bwd_copy(0).wait_send()


def body(
    n_dom,
    n_rep,
    profiles,
    pack_index,
    obs_slot,
    interp_weight,
    departures,
    w_in,
    b_in,
    w_mid,
    b_mid,
    w_out,
):
    feats, width = profiles.shape
    cap = pack_index.shape[3]
    slots = n_dom * cap
    obs = obs_slot.shape[1]
    hidden = w_in.shape[1]
    vmem = pl.BlockSpec(memory_space=pltpu.VMEM)
    operands = (
        profiles,
        pack_index.reshape(n_dom, cap),
        obs_slot,
        interp_weight,
        departures,
        w_in,
        b_in.reshape(1, hidden),
        w_mid,
        b_mid.reshape(1, hidden),
        w_out.T,
    )
    return pl.pallas_call(
        functools.partial(kernel, n_dom, n_rep),
        out_shape=pltpu.VMEM((feats, width // n_rep), F32),
        in_specs=[pl.BlockSpec(memory_space=pltpu.HBM)] * len(operands),
        out_specs=vmem,
        scratch_shapes=[
            *(pltpu.VMEM(operand.shape, operand.dtype) for operand in operands),
            pltpu.VMEM((n_rep, n_dom // n_rep, cap, feats), BF16),
            pltpu.VMEM((n_dom, cap, feats), BF16),
            pltpu.VMEM((n_rep, n_dom, cap), jnp.int32),
            pltpu.VMEM((obs, 2 * slots), BF16),
            pltpu.VMEM((2 * slots, obs), BF16),
            pltpu.VMEM((obs, hidden), F32),
            pltpu.VMEM((n_dom, cap, feats), BF16),
            pltpu.VMEM((n_dom, cap, feats), BF16),
            pltpu.SemaphoreType.DMA((len(operands),)),
            pltpu.SemaphoreType.DMA((n_rep,)),
            pltpu.SemaphoreType.DMA((n_rep,)),
            pltpu.SemaphoreType.DMA((n_rep,)),
            pltpu.SemaphoreType.DMA((n_dom,)),
            pltpu.SemaphoreType.DMA((n_dom,)),
            pltpu.SemaphoreType.DMA((n_dom,)),
            pltpu.SemaphoreType.DMA((n_dom,)),
        ],
        compiler_params=pltpu.CompilerParams(
            collective_id=0, has_side_effects=True, vmem_limit_bytes=62 * 1024 * 1024
        ),
    )(*(pltpu.with_memory_space_constraint(x, pltpu.HBM) for x in operands))


def solution(mesh):
    placed = (
        P(None, "dom"),
        P("dom", "rep", None, None),
        P(None, ("dom", "rep")),
        P(None, ("dom", "rep")),
        P(None, ("dom", "rep")),
        P(),
        P(),
        P(),
        P(),
        P(),
    )
    return jax.shard_map(
        functools.partial(body, mesh.shape["dom"], mesh.shape["rep"]),
        mesh=mesh,
        in_specs=placed,
        out_specs=P(None, ("dom", "rep")),
        check_vma=False,
    )
```
